256 devices in a mesh: seq: 32 (over z, x), head: 8 (over y, core).
Axes of the slice: x: 4, y: 4, z: 8, core: 2. Of those that a mesh axis runs over, the one named last changes fastest.
Arguments:
- query_rows: bfloat16 [24576, 4096], P('seq', 'head'), may hold values from -6 to 6
- key_rows: bfloat16 [24576, 4096], P('seq', 'head'), may hold values from -6 to 6
- value_rows: bfloat16 [24576, 4096], P('seq', 'head'), may hold values from -6 to 6
- grad_out: bfloat16 [24576, 4096], P('seq', 'head'), may hold values from -6 to 6
- doc_lengths: int32 [16], replicated, may hold values from 1 to 13440, as said below
Outputs:
- attended: bfloat16 [24576, 4096], P('seq', 'head')
- grad_query: bfloat16 [24576, 4096], P('seq', 'head')
- grad_key: bfloat16 [24576, 4096], P('seq', 'head')
- grad_value: bfloat16 [24576, 4096], P('seq', 'head')
The draws below stay inside these ranges and needn't reach their ends.
Inputs may be any that keep to these rules, and one draw needn't show every extreme that they name: `doc_lengths`: the 16 lengths sum to 24576; the last document is the longest, exactly 13440 long, and the first is longer than 768.
All inputs are finite; a program needn't handle non-finite values.
Results may differ from the reference program's by a relative error of at most 0.0043.
Values sent between devices are 32-bit elements; how exact they have to be, the bound alone decides.
A program may use at most 128 MiB of HBM per device.

```python
import jax
import jax.numpy as jnp
from jax import lax

DH = 128
HEADS = 32
T_DEV = 768
DOCS = 16
TOKENS = 24576
DOC_MOST = 13440


def draw_doc_lengths(key, part):
    rest = TOKENS - DOC_MOST
    pool = jnp.arange(T_DEV + 1, rest, dtype=jnp.int32)
    picks = jax.random.permutation(jax.random.fold_in(key, 11), pool)[:DOCS - 2]
    cuts = jnp.sort(picks)
    edges = jnp.concatenate([jnp.zeros((1,), jnp.int32), cuts, jnp.full((1,), rest, jnp.int32)])
    lengths = edges[1:] - edges[:-1]
    return jnp.concatenate([lengths, jnp.full((1,), DOC_MOST, jnp.int32)]).astype(jnp.int32)


def block_scale(key, extent, cuts, low, high):
    loudness = 1.0
    for position, shards_of in cuts:
        steps = jax.random.uniform(jax.random.fold_in(jax.random.fold_in(key, 6), position), (shards_of,), jnp.float32, low / len(cuts), high / len(cuts))
        loudness = loudness * jnp.repeat(jnp.exp(steps), extent[position] // shards_of).reshape((-1,) + (1,) * (len(extent) - 1 - position))
    return loudness


def bell_draw(key, shape, width, reach, cuts=(), kind=jnp.bfloat16):
    entries = width * jax.random.normal(key, shape, jnp.float32)
    if cuts:
        entries = entries * block_scale(key, shape, cuts, -0.22, 0.18)
    return jnp.clip(entries, -reach, reach).astype(kind)


def setup_inputs(seed: int = 0) -> dict:
    streams_of = jax.random.split(jax.random.key(seed), 6)
    return {
        "query_rows": bell_draw(streams_of[0], (TOKENS, HEADS * DH), 1.0, 6.0, ((0, 32), (1, 8))),
        "key_rows": bell_draw(streams_of[1], (TOKENS, HEADS * DH), 1.0, 6.0, ((0, 32), (1, 8))),
        "value_rows": bell_draw(streams_of[2], (TOKENS, HEADS * DH), 1.0, 6.0, ((0, 32), (1, 8))),
        "grad_out": bell_draw(streams_of[3], (TOKENS, HEADS * DH), 1.0, 6.0, ((0, 32), (1, 8))),
        "doc_lengths": draw_doc_lengths(jax.random.fold_in(streams_of[5], 71), 0),
    }


def doc_layout(doc_lengths, offset, count):
    starts = jnp.cumsum(doc_lengths, dtype=jnp.int32) - doc_lengths
    positions = offset + jnp.arange(count, dtype=jnp.int32)
    first_start = lax.optimization_barrier(jnp.max(jnp.where(starts[None, :] <= positions[:, None], starts[None, :], 0), axis=1))
    counts = (positions - first_start + 1).astype(jnp.float32)
    rowscale = 1.0 / jnp.sqrt(counts * DH)
    order = jnp.arange(count, dtype=jnp.int32)
    same_doc = (first_start[:, None] == first_start[None, :]) & (order[None, :] <= order[:, None])
    head_mask = (first_start < offset).astype(jnp.float32)
    tail_mask = (first_start == first_start[count - 1]).astype(jnp.float32)
    has_start = (first_start[count - 1] >= offset).astype(jnp.float32).reshape(1)
    return (rowscale, same_doc, head_mask, tail_mask, has_start)

def to_low(values):
    return lax.optimization_barrier(values.astype(jnp.bfloat16)).astype(jnp.float32)

def block_parts(block, query_blk, key_blk, value_blk, grad_blk, doc_lengths, block_size):
    highest = lax.Precision.HIGHEST
    offset = block * block_size
    rowscale, same_doc, head_mask, tail_mask, has_start = doc_layout(doc_lengths, offset, block_size)
    query_f = query_blk.astype(jnp.float32)
    key_f = key_blk.astype(jnp.float32)
    value_f = value_blk.astype(jnp.float32)
    grad_f = grad_blk.astype(jnp.float32)
    scores = jnp.where(same_doc[None], jnp.einsum('thd,shd->hts', query_f, key_f, precision=highest), 0.0)
    raw_grad = jnp.einsum('thd,shd->hts', grad_f, value_f, precision=highest)
    grad_scores = jnp.where(same_doc[None], raw_grad * rowscale[None, :, None], 0.0)
    scaled = rowscale[:, None, None] * grad_f
    return (rowscale, head_mask, tail_mask, has_start, query_f, key_f, value_f, to_low(scores), to_low(grad_scores), scaled, to_low(scaled))

def reference(query_rows, key_rows, value_rows, grad_out, doc_lengths):
    highest = lax.Precision.HIGHEST
    block_size = T_DEV
    block_count = TOKENS // block_size
    shape4 = (block_count, block_size, HEADS, DH)
    blocks = (jnp.arange(block_count, dtype=jnp.int32), query_rows.reshape(shape4), key_rows.reshape(shape4), value_rows.reshape(shape4), grad_out.reshape(shape4))

    def forward_step(state_in, inputs):
        block, query_blk, key_blk, value_blk, grad_blk = inputs
        rowscale, head_mask, tail_mask, has_start, query_f, key_f, value_f, scores_low, grad_low, scaled, scaled_low = block_parts(block, query_blk, key_blk, value_blk, grad_blk, doc_lengths, block_size)
        carried = jnp.einsum('thi,hij->thj', query_f, state_in, precision=highest)
        attended = rowscale[:, None, None] * (jnp.einsum('hts,shd->thd', scores_low, value_f, precision=highest) + head_mask[:, None, None] * carried)
        grad_query = jnp.einsum('hts,shd->thd', grad_low, key_f, precision=highest) + head_mask[:, None, None] * jnp.einsum('hij,thj->thi', state_in, scaled, precision=highest)
        tail_keys = key_f * tail_mask[:, None, None]
        state_out = jnp.where(has_start > 0.5, 0.0, state_in) + jnp.einsum('shi,shj->hij', tail_keys, value_f, precision=highest)
        return (state_out, (attended.astype(jnp.bfloat16), grad_query.astype(jnp.bfloat16)))

    def backward_step(grad_in, inputs):
        block, query_blk, key_blk, value_blk, grad_blk = inputs
        rowscale, head_mask, tail_mask, has_start, query_f, key_f, value_f, scores_low, grad_low, scaled, scaled_low = block_parts(block, query_blk, key_blk, value_blk, grad_blk, doc_lengths, block_size)
        grad_key = jnp.einsum('hts,thd->shd', grad_low, query_f, precision=highest) + tail_mask[:, None, None] * jnp.einsum('hij,shj->shi', grad_in, value_f, precision=highest)
        grad_value = jnp.einsum('hts,thd->shd', scores_low, scaled_low, precision=highest) + tail_mask[:, None, None] * jnp.einsum('shi,hij->shj', key_f, grad_in, precision=highest)
        head_queries = query_f * head_mask[:, None, None]
        grad_next = jnp.where(has_start > 0.5, 0.0, grad_in) + jnp.einsum('thi,thj->hij', head_queries, scaled, precision=highest)
        return (grad_next, (grad_key.astype(jnp.bfloat16), grad_value.astype(jnp.bfloat16)))
    zero_state = jnp.zeros((HEADS, DH, DH), jnp.float32)
    _, (attended, grad_query) = lax.scan(forward_step, zero_state, blocks)
    _, (grad_key, grad_value) = lax.scan(backward_step, zero_state, blocks, reverse=True)
    flat = (TOKENS, HEADS * DH)
    return (attended.reshape(flat), grad_query.reshape(flat), grad_key.reshape(flat), grad_value.reshape(flat))
```

```python
import functools

import jax
import jax.numpy as jnp
from jax import lax
from jax.experimental import pallas as pl
from jax.experimental.pallas import tpu as pltpu
from jax.sharding import PartitionSpec as P

MESH = pl.DeviceIdType.MESH
DH = 128
T = 768
NH = 4
DOCS = 16
NX = 4
QT = DH // NX
TB = 256
NB = T // TB
LAST_ROW = 3
REACH = 4
F32 = jnp.float32
BF16 = jnp.bfloat16


def dot_nn(a, b):
    return lax.dot_general(a, b, (((1,), (0,)), ((), ())), preferred_element_type=F32)


def dot_nt(a, b):
    return lax.dot_general(a, b, (((1,), (1,)), ((), ())), preferred_element_type=F32)


def dot_tn(a, b):
    return lax.dot_general(a, b, (((0,), (0,)), ((), ())), preferred_element_type=F32)


def split(a):
    high = a.astype(BF16)
    return high, (a - high.astype(F32)).astype(BF16)


def fused_kernel(
    len_hbm, q_hbm, k_hbm, v_hbm, g_hbm, o_att, o_gq, o_gk, o_gv,
    q, k, v, g, low, pa, pb, pc, pd, loc, p1, zs, zr, p3, st,
    rs_b, head_b, tail_b, tail_low, first_b,
    len_ref, len_sem, in_sem, s1, r1, sz, rz, s3, r3,
):
    seq = lax.axis_index("seq")
    z = seq // NX
    x = seq % NX
    offset = seq * T

    def goes_up(row, d):
        return (row >= 0) & ((row + d <= LAST_ROW) | ((row >= LAST_ROW) & (row + d <= 7)))

    def peer_x(d):
        return {"seq": z * NX + lax.rem(x + d, NX)}

    def peer_z(d):
        return {"seq": (z + d) * NX + x}

    lengths = pltpu.make_async_copy(len_hbm, len_ref, len_sem)
    lengths.start()

    barrier = pltpu.get_barrier_semaphore()
    for d in range(1, NX):
        pl.semaphore_signal(barrier, inc=1, device_id=peer_x(d), device_id_type=MESH)
    for d in range(1, REACH + 1):
        @pl.when(goes_up(z, d))
        def _():
            pl.semaphore_signal(barrier, inc=1, device_id=peer_z(d), device_id_type=MESH)

        @pl.when(goes_up(z - d, d))
        def _():
            pl.semaphore_signal(barrier, inc=1, device_id=peer_z(-d), device_id_type=MESH)

    def fetches(h):
        columns = pl.ds(pl.multiple_of(h * DH, DH), DH)
        return [
            pltpu.make_async_copy(src.at[:, columns], dst.at[h], in_sem.at[h, i])
            for i, (src, dst) in enumerate(((k_hbm, k), (v_hbm, v), (g_hbm, g), (q_hbm, q)))
        ]

    for h in range(NH):
        for copy in fetches(h):
            copy.start()

    lengths.wait()
    starts = [jnp.int32(0)]
    for j in range(DOCS - 1):
        starts.append(starts[-1] + len_ref[j])

    def last_start_before(limit):
        found = jnp.int32(0)
        for j in range(1, DOCS):
            found = jnp.where(starts[j] < limit, starts[j], found)
        return found

    row = z * (NX * T)
    has_start = [
        last_start_before(row + (i + 1) * T) >= row + i * T for i in range(NX)
    ]
    before_row = last_start_before(row)
    up_open = [True] + [before_row < row - (d - 1) * NX * T for d in range(2, REACH + 1)]
    down_open = [True] + [
        last_start_before(row + d * NX * T) < row + NX * T for d in range(2, REACH + 1)
    ]

    def first_of(shape, axis):
        place = lax.broadcasted_iota(jnp.int32, shape, axis)
        first = jnp.full(shape, -offset, jnp.int32)
        for j in range(1, DOCS):
            local = starts[j] - offset
            first = jnp.where(place >= local, local, first)
        return place, first

    place, first = first_of((T, DH), 0)
    scale = lax.rsqrt((place - first + 1).astype(F32) * DH)
    tail_from = last_start_before(offset + T) - offset
    tails = jnp.where(place >= tail_from, 1.0, 0.0)
    first_b[...] = first
    rs_b[...] = scale
    head_b[...] = jnp.where(first < 0, scale, 0.0)
    tail_b[...] = tails
    tail_low[...] = tails.astype(BF16)
    place_r, first_r = first_of((1, T), 1)
    scale_r = lax.rsqrt((place_r - first_r + 1).astype(F32) * DH)

    nz = jnp.where(z == LAST_ROW, 7, jnp.where(z < LAST_ROW, 3, 4))
    pl.semaphore_wait(barrier, NX - 1 + nz)

    def first_copy(h, d):
        target = lax.rem(x + d, NX)
        return pltpu.make_async_remote_copy(
            loc.at[h, :, pl.ds(pl.multiple_of(target * QT, QT), QT), :],
            p1.at[h, x],
            s1.at[h, d],
            r1.at[h, d],
            device_id=peer_x(d),
            device_id_type=MESH,
        )

    def row_copy(h, side, d):
        return pltpu.make_async_remote_copy(
            zs.at[h, side],
            zr.at[h, side, d - 1],
            sz.at[h, side, d - 1],
            rz.at[h, side, d - 1],
            device_id=peer_z(d if side == 0 else -d),
            device_id_type=MESH,
        )

    def last_copy(h, d):
        return pltpu.make_async_remote_copy(
            p3.at[h, lax.rem(x + d, NX)],
            st.at[h, :, pl.ds(pl.multiple_of(x * QT, QT), QT), :],
            s3.at[h, d],
            r3.at[h, d],
            device_id=peer_x(d),
            device_id_type=MESH,
        )

    mine = pl.ds(pl.multiple_of(x * QT, QT), QT)

    def states(h, carry):
        for copy in fetches(h):
            copy.wait()
        loc[h, 0] = dot_tn(k[h], v[h] * tail_low[...])
        gf = g[h].astype(F32)
        low[h] = (rs_b[...] * gf).astype(BF16)
        high_part, low_part = split(head_b[...] * gf)
        both = dot_tn(q[h], jnp.concatenate([high_part, low_part], axis=1))
        loc[h, 1] = both[:, :DH] + both[:, DH:]
        for d in range(1, NX):
            first_copy(h, d).start()
        p1[h, x] = loc[h, :, mine, :]
        return carry

    lax.fori_loop(0, NH, states, 0)

    def forward(h):
        for i in range(NB):
            n = TB * (i + 1)
            rows = pl.ds(TB * i, TB)
            over = lambda a: jnp.concatenate([a] * (n // DH), axis=1)
            s_at = lax.broadcasted_iota(jnp.int32, (TB, n), 1)
            t_at = lax.broadcasted_iota(jnp.int32, (TB, n), 0) + TB * i
            seen = (s_at >= over(first_b[rows, :])) & (s_at <= t_at)
            rs = rs_b[rows, :]
            scores = dot_nt(q[h, rows, :], k[h, :n, :])
            scores_low = jnp.where(seen, scores, 0.0).astype(BF16)
            pa[h, rows, :] = rs * dot_nn(scores_low, v[h, :n, :])
            raw = dot_nt(g[h, rows, :], v[h, :n, :])
            grad_low = jnp.where(seen, raw * over(rs), 0.0).astype(BF16)
            pb[h, rows, :] = dot_nn(grad_low, k[h, :n, :])

    def backward(h):
        for j in range(NB):
            m = T - TB * j
            lo = TB * j
            rows = pl.ds(lo, TB)
            s_at = lax.broadcasted_iota(jnp.int32, (TB, m), 0) + lo
            t_at = lax.broadcasted_iota(jnp.int32, (TB, m), 1) + lo
            seen = (s_at >= first_r[:, lo:]) & (s_at <= t_at)
            scores = dot_nt(k[h, rows, :], q[h, lo:, :])
            scores_low = jnp.where(seen, scores, 0.0).astype(BF16)
            pd[h, rows, :] = dot_nn(scores_low, low[h, lo:, :])
            raw = dot_nt(v[h, rows, :], g[h, lo:, :])
            grad_low = jnp.where(seen, raw * scale_r[:, lo:], 0.0).astype(BF16)
            pc[h, rows, :] = dot_nn(grad_low, q[h, lo:, :])

    def step_rows(h, carry):
        forward(h)
        for d in range(1, NX):
            first_copy(h, d).wait_recv()
        up = p1[h, 0, 0]
        down = p1[h, NX - 1, 1]
        for i in range(1, NX):
            up = p1[h, i, 0] + jnp.where(has_start[i], 0.0, up)
            back = NX - 1 - i
            down = p1[h, back, 1] + jnp.where(has_start[back], 0.0, down)
        zs[h, 0] = up
        zs[h, 1] = down
        for d in range(1, REACH + 1):
            @pl.when(goes_up(z, d))
            def _():
                row_copy(h, 0, d).start()

            @pl.when(goes_up(z - d, d))
            def _():
                row_copy(h, 1, d).start()
        return carry

    lax.fori_loop(0, NH, step_rows, 0)

    def step_last(h, carry):
        backward(h)
        up = jnp.zeros((QT, DH), F32)
        down = jnp.zeros((QT, DH), F32)
        for d in range(1, REACH + 1):
            @pl.when(goes_up(z - d, d))
            def _():
                row_copy(h, 0, d).wait_recv()

            @pl.when(goes_up(z, d))
            def _():
                row_copy(h, 1, d).wait_recv()

            up = up + jnp.where(goes_up(z - d, d) & up_open[d - 1], zr[h, 0, d - 1], 0.0)
            down = down + jnp.where(goes_up(z, d) & down_open[d - 1], zr[h, 1, d - 1], 0.0)
        for i in range(NX):
            p3[h, i, 0] = up
            up = p1[h, i, 0] + jnp.where(has_start[i], 0.0, up)
            back = NX - 1 - i
            p3[h, back, 1] = down
            down = p1[h, back, 1] + jnp.where(has_start[back], 0.0, down)
        for d in range(1, NX):
            last_copy(h, d).start()
        st[h, :, mine, :] = p3[h, x]
        return carry

    lax.fori_loop(0, NH, step_last, 0)

    def finish(h, carry):
        for d in range(1, NX):
            last_copy(h, d).wait_recv()
        kv_high, kv_low = split(st[h, 0])
        qg_high, qg_low = split(st[h, 1])
        columns = pl.ds(pl.multiple_of(h * DH, DH), DH)
        kv_wide = jnp.concatenate([kv_high, kv_low], axis=1)
        kv_tall = jnp.concatenate([kv_high, kv_low], axis=0)
        qg_wide = jnp.concatenate([qg_high, qg_low], axis=1)
        qg_tall = jnp.concatenate([qg_high, qg_low], axis=0)
        for i in range(NB):
            rows = pl.ds(TB * i, TB)
            twice = lambda a: jnp.concatenate([a[h, rows, :]] * 2, axis=1)
            head = head_b[rows, :]
            tail = tail_b[rows, :]
            o_att[rows, columns] = (pa[h, rows, :] + head * dot_nn(twice(q), kv_tall)).astype(BF16)
            o_gq[rows, columns] = (pb[h, rows, :] + head * dot_nt(twice(g), kv_wide)).astype(BF16)
            o_gk[rows, columns] = (pc[h, rows, :] + tail * dot_nt(twice(v), qg_wide)).astype(BF16)
            o_gv[rows, columns] = (pd[h, rows, :] + tail * dot_nn(twice(k), qg_tall)).astype(BF16)
        return carry

    lax.fori_loop(0, NH, finish, 0)

    def drain(h, carry):
        for d in range(1, NX):
            first_copy(h, d).wait_send()
            last_copy(h, d).wait_send()
        for d in range(1, REACH + 1):
            @pl.when(goes_up(z, d))
            def _():
                row_copy(h, 0, d).wait_send()

            @pl.when(goes_up(z - d, d))
            def _():
                row_copy(h, 1, d).wait_send()
        return carry

    lax.fori_loop(0, NH, drain, 0)


def store_kernel(*refs):
    ins, outs, sem = refs[:4], refs[4:8], refs[8]
    copies = [pltpu.make_async_copy(a, b, sem.at[i]) for i, (a, b) in enumerate(zip(ins, outs))]
    for copy in copies:
        copy.start()
    for copy in copies:
        copy.wait()


def per_device(query_rows, key_rows, value_rows, grad_out, doc_lengths):
    whole = pl.BlockSpec(memory_space=pltpu.HBM)
    in_vmem = pl.BlockSpec(memory_space=pltpu.VMEM)
    wide = (T, NH * DH)
    heads = (NH, T, DH)
    dma = pltpu.SemaphoreType.DMA
    results = pl.pallas_call(
        fused_kernel,
        name="attend",
        out_shape=[pltpu.VMEM(wide, BF16)] * 4,
        in_specs=[whole] * 5,
        out_specs=[in_vmem] * 4,
        scratch_shapes=[pltpu.VMEM(heads, BF16)] * 5
        + [pltpu.VMEM(heads, F32)] * 4
        + [
            pltpu.VMEM((NH, 2, DH, DH), F32),
            pltpu.VMEM((NH, NX, 2, QT, DH), F32),
            pltpu.VMEM((NH, 2, QT, DH), F32),
            pltpu.VMEM((NH, 2, REACH, QT, DH), F32),
            pltpu.VMEM((NH, NX, 2, QT, DH), F32),
            pltpu.VMEM((NH, 2, DH, DH), F32),
            pltpu.VMEM((T, DH), F32),
            pltpu.VMEM((T, DH), F32),
            pltpu.VMEM((T, DH), F32),
            pltpu.VMEM((T, DH), BF16),
            pltpu.VMEM((T, DH), jnp.int32),
            pltpu.SMEM((DOCS,), jnp.int32),
            dma,
            dma((NH, 4)),
            dma((NH, NX)),
            dma((NH, NX)),
            dma((NH, 2, REACH)),
            dma((NH, 2, REACH)),
            dma((NH, NX)),
            dma((NH, NX)),
        ],
        compiler_params=pltpu.CompilerParams(
            collective_id=0, has_side_effects=True, vmem_limit_bytes=40 << 20
        ),
    )(*(
        pltpu.with_memory_space_constraint(a, pltpu.HBM)
        for a in (doc_lengths, query_rows, key_rows, value_rows, grad_out)
    ))
    return tuple(
        pl.pallas_call(
            store_kernel,
            name="store",
            out_shape=[jax.ShapeDtypeStruct(wide, BF16)] * 4,
            in_specs=[in_vmem] * 4,
            out_specs=[whole] * 4,
            scratch_shapes=[dma((4,))],
            compiler_params=pltpu.CompilerParams(vmem_limit_bytes=8 << 20),
        )(*results)
    )


def solution(mesh):
    placed = (P("seq", "head"), P("seq", "head"), P("seq", "head"), P("seq", "head"), P())
    return jax.shard_map(
        per_device,
        mesh=mesh,
        in_specs=placed,
        out_specs=(P("seq", "head"), P("seq", "head"), P("seq", "head"), P("seq", "head")),
        check_vma=False,
    )
```

```python
import functools

import jax
import jax.numpy as jnp
from jax import lax
from jax.experimental import pallas as pl
from jax.experimental.pallas import tpu as pltpu
from jax.sharding import PartitionSpec as P

MESH = pl.DeviceIdType.MESH
DH = 128
T = 768
NH = 4
DOCS = 16
NX = 4
QT = DH // NX
TB = 256
NB = T // TB
FIRST = 2
FAR_FIRST = (2, 1, 3)
LAST_ROW = 3
NG = 4
F32 = jnp.float32
BF16 = jnp.bfloat16


def dot_nn(a, b):
    return lax.dot_general(a, b, (((1,), (0,)), ((), ())), preferred_element_type=F32)


def dot_nt(a, b):
    return lax.dot_general(a, b, (((1,), (1,)), ((), ())), preferred_element_type=F32)


def dot_tn(a, b):
    return lax.dot_general(a, b, (((0,), (0,)), ((), ())), preferred_element_type=F32)


def split(a):
    high = a.astype(BF16)
    return high, (a - high.astype(F32)).astype(BF16)


def fused_kernel(
    len_hbm, q_hbm, k_hbm, v_hbm, g_hbm, o_att, o_gq, o_gk, o_gv,
    ins, low, pa, pb, pc, pd, kvs, qgs, loc, p1, zs, zr, zx, p3, st,
    rs_b, head_b, tail_b, tail_low, first_b,
    len_ref, len_sem, above_sem, in_sem, s1, r1, sz, rz, sx, rx, sw, rw, s3, s3_part, r3,
):
    q, k, v, g = (ins.at[:, i] for i in range(4))
    seq = lax.axis_index("seq")
    z = seq // NX
    x = seq % NX
    offset = seq * T
    base = (z // NG) * NG
    r = z - base
    below = z == NG - 1
    above = z == NG
    begins = below & (x >= NX - 2)

    def peer_x(d):
        return {"seq": z * NX + lax.rem(x + d, NX)}

    def peer_row(d):
        return lax.rem(r + d, NG)

    def peer_z(d):
        return {"seq": (base + peer_row(d)) * NX + x}

    def wait_bytes(ref, sem):
        pltpu.make_async_copy(ref, ref, sem).wait()

    lengths = pltpu.make_async_copy(len_hbm, len_ref, len_sem)
    lengths.start()

    barrier = pltpu.get_barrier_semaphore()
    for d in range(1, NX):
        pl.semaphore_signal(barrier, inc=1, device_id=peer_x(d), device_id_type=MESH)
    for d in range(1, NG):
        @pl.when(peer_row(d) > r)
        def _():
            pl.semaphore_signal(barrier, inc=1, device_id=peer_z(d), device_id_type=MESH)

    @pl.when(below)
    def _():
        up = {"seq": NG * NX + x}
        pl.semaphore_signal(barrier, inc=1, device_id=up, device_id_type=MESH)

    @pl.when(begins)
    def _():
        for d in range(1, NX):
            beside = {"seq": NG * NX + lax.rem(x + d, NX)}
            pl.semaphore_signal(barrier, inc=1, device_id=beside, device_id_type=MESH)

    def fetches(h):
        columns = pl.ds(pl.multiple_of(h * DH, DH), DH)
        return [
            pltpu.make_async_copy(src.at[:, columns], ins.at[h, i], in_sem.at[h])
            for i, src in enumerate((q_hbm, k_hbm, v_hbm, g_hbm))
        ]

    for h in range(NH):
        for copy in fetches(h):
            copy.start()

    lengths.wait()
    starts = [jnp.int32(0)]
    for j in range(DOCS - 1):
        starts.append(starts[-1] + len_ref[j])

    def last_start_before(limit):
        found = jnp.int32(0)
        for j in range(1, DOCS):
            found = jnp.where(starts[j] < limit, starts[j], found)
        return found

    row = z * (NX * T)
    has_start = [
        last_start_before(row + (i + 1) * T) >= row + i * T for i in range(NX)
    ]
    before_row = last_start_before(row)
    up_open = [before_row < (base + i + 1) * NX * T for i in range(NG)]
    down_open = [last_start_before((base + i) * NX * T) < row + NX * T for i in range(NG)]

    def first_of(place):
        first = jnp.full(place.shape, -offset, jnp.int32)
        for j in range(1, DOCS):
            local = starts[j] - offset
            first = jnp.where(place >= local, local, first)
        return first, lax.rsqrt((place - first + 1).astype(F32) * DH)

    chunk_start = []
    for c in range(NB):
        from_here = last_start_before(offset + TB * (c + 1)) - offset
        chunk_start.append(from_here >= TB * c)
        for top in range(TB * c, TB * (c + 1), DH):
            rows = pl.ds(top, DH)
            place = lax.broadcasted_iota(jnp.int32, (DH, DH), 0) + top
            first, scale = first_of(place)
            first_b[rows, :] = first
            rs_b[rows, :] = scale
            head_b[rows, :] = jnp.where(first < TB * c, scale, 0.0)
            tails = jnp.where(place >= from_here, 1.0, 0.0)
            tail_b[rows, :] = tails
            tail_low[rows, :] = tails.astype(BF16)

    from_below = jnp.where(above, jnp.where(x >= NX - 2, 2, 3), r)
    pl.semaphore_wait(barrier, NX - 1 + from_below)
    for d in range(1, NG):
        @pl.when(peer_row(d) < r)
        def _():
            pl.semaphore_signal(above_sem, inc=1, device_id=peer_z(d), device_id_type=MESH)

    @pl.when(above)
    def _():
        down = {"seq": (NG - 1) * NX + x}
        pl.semaphore_signal(above_sem, inc=1, device_id=down, device_id_type=MESH)

    def first_copy(h, d):
        target = lax.rem(x + d, NX)
        return pltpu.make_async_remote_copy(
            loc.at[h, :, pl.ds(pl.multiple_of(target * QT, QT), QT), :],
            p1.at[h, x],
            s1,
            r1.at[h],
            device_id=peer_x(d),
            device_id_type=MESH,
        )

    def row_copy(h, d):
        return pltpu.make_async_remote_copy(
            zs.at[h, jnp.where(peer_row(d) > r, 1, 0)],
            zr.at[h, r],
            sz,
            rz.at[h],
            device_id=peer_z(d),
            device_id_type=MESH,
        )

    def over_copy(h):
        return pltpu.make_async_remote_copy(
            zs.at[h, 1:3],
            zx.at[h],
            sx,
            rx.at[h],
            device_id={"seq": NG * NX + x},
            device_id_type=MESH,
        )

    def under_copy(h, i):
        return pltpu.make_async_remote_copy(
            zx.at[h, i],
            st.at[h, 1, mine, :],
            sw,
            rw.at[h],
            device_id={"seq": (NG - 1) * NX + NX - 2 + i},
            device_id_type=MESH,
        )

    def last_copy(h, d):
        return pltpu.make_async_remote_copy(
            p3.at[h, lax.rem(x + d, NX)],
            st.at[h, :, mine, :],
            s3,
            r3.at[h],
            device_id=peer_x(d),
            device_id_type=MESH,
        )

    def last_part(h, d):
        return pltpu.make_async_remote_copy(
            p3.at[h, lax.rem(x + d, NX), 0],
            st.at[h, 0, mine, :],
            s3_part,
            r3.at[h],
            device_id=peer_x(d),
            device_id_type=MESH,
        )

    mine = pl.ds(pl.multiple_of(x * QT, QT), QT)

    def states(h, carry):
        wait_bytes(ins.at[h], in_sem.at[h])
        for c in range(NB):
            rows = pl.ds(TB * c, TB)
            kvs[h, c] = dot_tn(k[h, rows, :], v[h, rows, :] * tail_low[rows, :])
            gf = g[h, rows, :].astype(F32)
            low[h, rows, :] = (rs_b[rows, :] * gf).astype(BF16)
            high_part, low_part = split(head_b[rows, :] * gf)
            both = dot_tn(q[h, rows, :], jnp.concatenate([high_part, low_part], axis=1))
            qgs[h, c] = both[:, :DH] + both[:, DH:]
        up = kvs[h, 0]
        down = qgs[h, NB - 1]
        for c in range(1, NB):
            up = kvs[h, c] + jnp.where(chunk_start[c], 0.0, up)
            back = NB - 1 - c
            down = qgs[h, back] + jnp.where(chunk_start[back], 0.0, down)
        loc[h, 0] = up
        loc[h, 1] = down
        for d in FAR_FIRST:
            first_copy(h, d).start()
        p1[h, x] = loc[h, :, mine, :]
        return carry

    lax.fori_loop(0, NH, states, 0)

    def inside(h):
        for c in range(NB):
            rows = pl.ds(TB * c, TB)
            qc, kc, vc, gc = (a[h, rows, :] for a in (q, k, v, g))
            over = lambda a: jnp.concatenate([a] * (TB // DH), axis=1)
            high = lax.broadcasted_iota(jnp.int32, (TB, TB), 0)
            wide = lax.broadcasted_iota(jnp.int32, (TB, TB), 1)
            seen = (wide + TB * c >= over(first_b[rows, :])) & (wide <= high)
            rs = rs_b[rows, :]
            scores = jnp.where(seen, dot_nt(qc, kc), 0.0).astype(BF16)
            grads = jnp.where(seen, dot_nt(gc, vc) * over(rs), 0.0).astype(BF16)
            pa[h, rows, :] = rs * dot_nn(scores, vc)
            pb[h, rows, :] = dot_nn(grads, kc)
            pd[h, rows, :] = dot_tn(scores, low[h, rows, :])
            pc[h, rows, :] = dot_tn(grads, qc)

    def step_rows(h, carry):
        wait_bytes(p1.at[h, 1:], r1.at[h])
        up = p1[h, 0, 0]
        down = p1[h, NX - 1, 1]
        for i in range(1, NX):
            up = p1[h, i, 0] + jnp.where(has_start[i], 0.0, up)
            back = NX - 1 - i
            down = p1[h, back, 1] + jnp.where(has_start[back], 0.0, down)
        zs[h, 0] = down
        zs[h, 1] = up
        zs[h, 2] = p1[h, NX - 1, 1]

        @pl.when(below)
        def _():
            over_copy(h).start()

        @pl.when(above)
        def _():
            wait_bytes(zx.at[h], rx.at[h])
            zs[h, 1] = zs[h, 1] + zx[h, 0]

        for d in range(1, NG):
            row_copy(h, d).start()
        return carry

    def inner(h, carry):
        inside(h)
        return carry

    lax.fori_loop(0, FIRST, inner, 0)

    @pl.when(below | (r < NG - 1))
    def _():
        pl.semaphore_wait(above_sem, NG - 1 - r + jnp.where(below, 1, 0))

    lax.fori_loop(0, NH, step_rows, 0)
    lax.fori_loop(FIRST, NH, inner, 0)

    def step_last(h, carry):
        wait_bytes(zr.at[h, 1:], rz.at[h])
        up = jnp.where(above, zx[h, 0], 0.0)
        down = jnp.zeros((QT, DH), F32)
        for i in range(NG):
            up = up + jnp.where((r > i) & up_open[i], zr[h, i], 0.0)
            down = down + jnp.where((r < i) & down_open[i], zr[h, i], 0.0)
        for i in range(NX):
            p3[h, i, 0] = up
            up = p1[h, i, 0] + jnp.where(has_start[i], 0.0, up)
            back = NX - 1 - i
            p3[h, back, 1] = down
            down = p1[h, back, 1] + jnp.where(has_start[back], 0.0, down)

        @pl.when(above)
        def _():
            zx[h, 0] = down + zx[h, 1]
            zx[h, 1] = down
            for i in range(2):
                under_copy(h, i).start()

        for d in FAR_FIRST:
            part = below & (lax.rem(x + d, NX) >= NX - 2)

            @pl.when(~part)
            def _():
                last_copy(h, d).start()

            @pl.when(part)
            def _():
                last_part(h, d).start()

        st[h, 0, mine, :] = p3[h, x, 0]

        @pl.when(~begins)
        def _():
            st[h, 1, mine, :] = p3[h, x, 1]

        return carry

    lax.fori_loop(0, NH, step_last, 0)

    wait_bytes(p1.at[:, 1:], s1)
    wait_bytes(zr.at[:, 1:], sz)

    @pl.when(below)
    def _():
        wait_bytes(zx, sx)

    def finish(h, carry):
        @pl.when(begins)
        def _():
            wait_bytes(p3.at[h, 1:, 0], r3.at[h])
            wait_bytes(st.at[h, 1], rw.at[h])

        @pl.when(~begins)
        def _():
            wait_bytes(p3.at[h, 1:], r3.at[h])

        columns = pl.ds(pl.multiple_of(h * DH, DH), DH)
        kv_in = [st[h, 0]]
        for c in range(NB - 1):
            kv_in.append(kvs[h, c] + jnp.where(chunk_start[c], 0.0, kv_in[-1]))
        qg_in = [st[h, 1]]
        for c in range(NB - 1, 0, -1):
            qg_in.insert(0, qgs[h, c] + jnp.where(chunk_start[c], 0.0, qg_in[0]))
        for c in range(NB):
            rows = pl.ds(TB * c, TB)
            kv_parts = split(kv_in[c])
            qg_parts = split(qg_in[c])
            kv_wide, kv_tall = (jnp.concatenate(kv_parts, axis=i) for i in (1, 0))
            qg_wide, qg_tall = (jnp.concatenate(qg_parts, axis=i) for i in (1, 0))
            twice = lambda a: jnp.concatenate([a[h, rows, :]] * 2, axis=1)
            head = head_b[rows, :]
            tail = tail_b[rows, :]
            o_att[rows, columns] = (pa[h, rows, :] + head * dot_nn(twice(q), kv_tall)).astype(BF16)
            o_gq[rows, columns] = (pb[h, rows, :] + head * dot_nt(twice(g), kv_wide)).astype(BF16)
            o_gk[rows, columns] = (pc[h, rows, :] + tail * dot_nt(twice(v), qg_wide)).astype(BF16)
            o_gv[rows, columns] = (pd[h, rows, :] + tail * dot_nn(twice(k), qg_tall)).astype(BF16)
        return carry

    lax.fori_loop(0, NH, finish, 0)

    @pl.when(~below)
    def _():
        wait_bytes(p3.at[:, 1:], s3)

    @pl.when(begins)
    def _():
        wait_bytes(p3.at[:, 2:], s3)
        wait_bytes(p3.at[:, 0, 0], s3_part)

    @pl.when(below & ~begins)
    def _():
        wait_bytes(p3.at[:, 0], s3)
        wait_bytes(p3.at[:, 2:, 0], s3_part)

    @pl.when(above)
    def _():
        wait_bytes(zx, sw)


def store_kernel(*refs):
    ins, outs, sem = refs[:4], refs[4:8], refs[8]
    copies = [pltpu.make_async_copy(a, b, sem.at[i]) for i, (a, b) in enumerate(zip(ins, outs))]
    for copy in copies:
        copy.start()
    for copy in copies:
        copy.wait()


def per_device(query_rows, key_rows, value_rows, grad_out, doc_lengths):
    whole = pl.BlockSpec(memory_space=pltpu.HBM)
    in_vmem = pl.BlockSpec(memory_space=pltpu.VMEM)
    wide = (T, NH * DH)
    heads = (NH, T, DH)
    dma = pltpu.SemaphoreType.DMA
    results = pl.pallas_call(
        fused_kernel,
        name="attend",
        out_shape=[pltpu.VMEM(wide, BF16)] * 4,
        in_specs=[whole] * 5,
        out_specs=[in_vmem] * 4,
        scratch_shapes=[pltpu.VMEM((NH, 4, T, DH), BF16), pltpu.VMEM(heads, BF16)]
        + [pltpu.VMEM(heads, F32)] * 4
        + [
            pltpu.VMEM((NH, NB, DH, DH), F32),
            pltpu.VMEM((NH, NB, DH, DH), F32),
            pltpu.VMEM((NH, 2, DH, DH), F32),
            pltpu.VMEM((NH, NX, 2, QT, DH), F32),
            pltpu.VMEM((NH, 3, QT, DH), F32),
            pltpu.VMEM((NH, NG, QT, DH), F32),
            pltpu.VMEM((NH, 2, QT, DH), F32),
            pltpu.VMEM((NH, NX, 2, QT, DH), F32),
            pltpu.VMEM((NH, 2, DH, DH), F32),
            pltpu.VMEM((T, DH), F32),
            pltpu.VMEM((T, DH), F32),
            pltpu.VMEM((T, DH), F32),
            pltpu.VMEM((T, DH), BF16),
            pltpu.VMEM((T, DH), jnp.int32),
            pltpu.SMEM((DOCS,), jnp.int32),
            dma,
            pltpu.SemaphoreType.REGULAR,
            dma((NH,)),
            dma,
            dma((NH,)),
            dma,
            dma((NH,)),
            dma,
            dma((NH,)),
            dma,
            dma((NH,)),
            dma,
            dma,
            dma((NH,)),
        ],
        compiler_params=pltpu.CompilerParams(
            collective_id=0, has_side_effects=True, vmem_limit_bytes=40 << 20
        ),
    )(*(
        pltpu.with_memory_space_constraint(a, pltpu.HBM)
        for a in (doc_lengths, query_rows, key_rows, value_rows, grad_out)
    ))
    return tuple(
        pl.pallas_call(
            store_kernel,
            name="store",
            out_shape=[jax.ShapeDtypeStruct(wide, BF16)] * 4,
            in_specs=[in_vmem] * 4,
            out_specs=[whole] * 4,
            scratch_shapes=[dma((4,))],
            compiler_params=pltpu.CompilerParams(vmem_limit_bytes=8 << 20),
        )(*results)
    )


def solution(mesh):
    placed = (P("seq", "head"), P("seq", "head"), P("seq", "head"), P("seq", "head"), P())
    return jax.shard_map(
        per_device,
        mesh=mesh,
        in_specs=placed,
        out_specs=(P("seq", "head"), P("seq", "head"), P("seq", "head"), P("seq", "head")),
        check_vma=False,
    )
```

```python
import functools

import jax
import jax.numpy as jnp
from jax import lax
from jax.experimental import pallas as pl
from jax.experimental.pallas import tpu as pltpu
from jax.sharding import PartitionSpec as P

MESH = pl.DeviceIdType.MESH
DH = 128
T = 768
NH = 4
DOCS = 16
NX = 4
QT = DH // NX
TB = 256
NB = T // TB
FIRST = 3
FAR_FIRST = (2, 1, 3)
LAST_ROW = 3
NG = 4
F32 = jnp.float32
BF16 = jnp.bfloat16


def dot_nn(a, b):
    return lax.dot_general(a, b, (((1,), (0,)), ((), ())), preferred_element_type=F32)


def dot_nt(a, b):
    return lax.dot_general(a, b, (((1,), (1,)), ((), ())), preferred_element_type=F32)


def dot_tn(a, b):
    return lax.dot_general(a, b, (((0,), (0,)), ((), ())), preferred_element_type=F32)


def split(a):
    high = a.astype(BF16)
    return high, (a - high.astype(F32)).astype(BF16)


def fused_kernel(
    len_hbm, q_hbm, k_hbm, v_hbm, g_hbm, o_att, o_gq, o_gk, o_gv,
    ins, low, pa, pb, pc, pd, kvs, qgs, loc, p1, zs, zr, zx, p3, st,
    rs_b, head_b, tail_b, tail_low, first_b,
    len_ref, len_sem, above_sem, in_sem, s1, r1, sz, rz, sx, rx, sw, rw, s3, s3_part, r3,
):
    q, k, v, g = (ins.at[:, i] for i in range(4))
    seq = lax.axis_index("seq")
    z = seq // NX
    x = seq % NX
    offset = seq * T
    base = (z // NG) * NG
    r = z - base
    below = z == NG - 1
    above = z == NG
    begins = below & (x >= NX - 2)

    def peer_x(d):
        return {"seq": z * NX + lax.rem(x + d, NX)}

    def peer_row(d):
        return lax.rem(r + d, NG)

    def peer_z(d):
        return {"seq": (base + peer_row(d)) * NX + x}

    def wait_bytes(ref, sem):
        pltpu.make_async_copy(ref, ref, sem).wait()

    lengths = pltpu.make_async_copy(len_hbm, len_ref, len_sem)
    lengths.start()

    barrier = pltpu.get_barrier_semaphore()
    for d in range(1, NX):
        pl.semaphore_signal(barrier, inc=1, device_id=peer_x(d), device_id_type=MESH)
    for d in range(1, NG):
        @pl.when(peer_row(d) > r)
        def _():
            pl.semaphore_signal(barrier, inc=1, device_id=peer_z(d), device_id_type=MESH)

    @pl.when(below)
    def _():
        up = {"seq": NG * NX + x}
        pl.semaphore_signal(barrier, inc=1, device_id=up, device_id_type=MESH)

    @pl.when(begins)
    def _():
        for d in range(1, NX):
            beside = {"seq": NG * NX + lax.rem(x + d, NX)}
            pl.semaphore_signal(barrier, inc=1, device_id=beside, device_id_type=MESH)

    def fetches(h):
        columns = pl.ds(pl.multiple_of(h * DH, DH), DH)
        return [
            pltpu.make_async_copy(src.at[:, columns], ins.at[h, i], in_sem.at[h])
            for i, src in enumerate((q_hbm, k_hbm, v_hbm, g_hbm))
        ]

    for h in range(NH):
        for copy in fetches(h):
            copy.start()

    lengths.wait()
    starts = [jnp.int32(0)]
    for j in range(DOCS - 1):
        starts.append(starts[-1] + len_ref[j])

    def last_start_before(limit):
        found = jnp.int32(0)
        for j in range(1, DOCS):
            found = jnp.where(starts[j] < limit, starts[j], found)
        return found

    row = z * (NX * T)
    has_start = [
        last_start_before(row + (i + 1) * T) >= row + i * T for i in range(NX)
    ]
    before_row = last_start_before(row)
    up_open = [before_row < (base + i + 1) * NX * T for i in range(NG)]
    down_open = [last_start_before((base + i) * NX * T) < row + NX * T for i in range(NG)]

    def first_of(place):
        first = jnp.full(place.shape, -offset, jnp.int32)
        for j in range(1, DOCS):
            local = starts[j] - offset
            first = jnp.where(place >= local, local, first)
        return first, lax.rsqrt((place - first + 1).astype(F32) * DH)

    chunk_start = []
    for c in range(NB):
        from_here = last_start_before(offset + TB * (c + 1)) - offset
        chunk_start.append(from_here >= TB * c)
        for top in range(TB * c, TB * (c + 1), DH):
            rows = pl.ds(top, DH)
            place = lax.broadcasted_iota(jnp.int32, (DH, DH), 0) + top
            first, scale = first_of(place)
            first_b[rows, :] = first
            rs_b[rows, :] = scale
            head_b[rows, :] = jnp.where(first < TB * c, scale, 0.0)
            tails = jnp.where(place >= from_here, 1.0, 0.0)
            tail_b[rows, :] = tails
            tail_low[rows, :] = tails.astype(BF16)

    from_below = jnp.where(above, jnp.where(x >= NX - 2, 2, 3), r)
    pl.semaphore_wait(barrier, NX - 1 + from_below)
    for d in range(1, NG):
        @pl.when(peer_row(d) < r)
        def _():
            pl.semaphore_signal(above_sem, inc=1, device_id=peer_z(d), device_id_type=MESH)

    @pl.when(above)
    def _():
        down = {"seq": (NG - 1) * NX + x}
        pl.semaphore_signal(above_sem, inc=1, device_id=down, device_id_type=MESH)

    def first_copy(h, d):
        target = lax.rem(x + d, NX)
        return pltpu.make_async_remote_copy(
            loc.at[h, :, pl.ds(pl.multiple_of(target * QT, QT), QT), :],
            p1.at[h, x],
            s1,
            r1.at[h],
            device_id=peer_x(d),
            device_id_type=MESH,
        )

    def row_copy(h, d):
        return pltpu.make_async_remote_copy(
            zs.at[h, jnp.where(peer_row(d) > r, 1, 0)],
            zr.at[h, r],
            sz,
            rz.at[h],
            device_id=peer_z(d),
            device_id_type=MESH,
        )

    def over_copy(h):
        return pltpu.make_async_remote_copy(
            zs.at[h, 1:3],
            zx.at[h],
            sx,
            rx.at[h],
            device_id={"seq": NG * NX + x},
            device_id_type=MESH,
        )

    def under_copy(h, i):
        return pltpu.make_async_remote_copy(
            zx.at[h, i],
            st.at[h, 1, mine, :],
            sw,
            rw.at[h],
            device_id={"seq": (NG - 1) * NX + NX - 2 + i},
            device_id_type=MESH,
        )

    def last_copy(h, d):
        return pltpu.make_async_remote_copy(
            p3.at[h, lax.rem(x + d, NX)],
            st.at[h, :, mine, :],
            s3,
            r3.at[h],
            device_id=peer_x(d),
            device_id_type=MESH,
        )

    def last_part(h, d):
        return pltpu.make_async_remote_copy(
            p3.at[h, lax.rem(x + d, NX), 0],
            st.at[h, 0, mine, :],
            s3_part,
            r3.at[h],
            device_id=peer_x(d),
            device_id_type=MESH,
        )

    mine = pl.ds(pl.multiple_of(x * QT, QT), QT)

    def states(h, carry):
        wait_bytes(ins.at[h], in_sem.at[h])
        for c in range(NB):
            rows = pl.ds(TB * c, TB)
            kvs[h, c] = dot_tn(k[h, rows, :], v[h, rows, :] * tail_low[rows, :])
            gf = g[h, rows, :].astype(F32)
            low[h, rows, :] = (rs_b[rows, :] * gf).astype(BF16)
            high_part, low_part = split(head_b[rows, :] * gf)
            both = dot_tn(q[h, rows, :], jnp.concatenate([high_part, low_part], axis=1))
            qgs[h, c] = both[:, :DH] + both[:, DH:]
        up = kvs[h, 0]
        down = qgs[h, NB - 1]
        for c in range(1, NB):
            up = kvs[h, c] + jnp.where(chunk_start[c], 0.0, up)
            back = NB - 1 - c
            down = qgs[h, back] + jnp.where(chunk_start[back], 0.0, down)
        loc[h, 0] = up
        loc[h, 1] = down
        for d in FAR_FIRST:
            first_copy(h, d).start()
        p1[h, x] = loc[h, :, mine, :]
        return carry

    lax.fori_loop(0, NH, states, 0)

    def inside(h):
        for c in range(NB):
            rows = pl.ds(TB * c, TB)
            qc, kc, vc, gc = (a[h, rows, :] for a in (q, k, v, g))
            over = lambda a: jnp.concatenate([a] * (TB // DH), axis=1)
            high = lax.broadcasted_iota(jnp.int32, (TB, TB), 0)
            wide = lax.broadcasted_iota(jnp.int32, (TB, TB), 1)
            seen = (wide + TB * c >= over(first_b[rows, :])) & (wide <= high)
            rs = rs_b[rows, :]
            scores = jnp.where(seen, dot_nt(qc, kc), 0.0).astype(BF16)
            grads = jnp.where(seen, dot_nt(gc, vc) * over(rs), 0.0).astype(BF16)
            pa[h, rows, :] = rs * dot_nn(scores, vc)
            pb[h, rows, :] = dot_nn(grads, kc)
            pd[h, rows, :] = dot_tn(scores, low[h, rows, :])
            pc[h, rows, :] = dot_tn(grads, qc)

    def step_rows(h, carry):
        wait_bytes(p1.at[h, 1:], r1.at[h])
        up = p1[h, 0, 0]
        down = p1[h, NX - 1, 1]
        for i in range(1, NX):
            up = p1[h, i, 0] + jnp.where(has_start[i], 0.0, up)
            back = NX - 1 - i
            down = p1[h, back, 1] + jnp.where(has_start[back], 0.0, down)
        zs[h, 0] = down
        zs[h, 1] = up
        zs[h, 2] = p1[h, NX - 1, 1]

        @pl.when(below)
        def _():
            over_copy(h).start()

        @pl.when(above)
        def _():
            wait_bytes(zx.at[h], rx.at[h])
            zs[h, 1] = zs[h, 1] + zx[h, 0]

        for d in range(1, NG):
            row_copy(h, d).start()
        return carry

    def inner(h, carry):
        inside(h)
        return carry

    lax.fori_loop(0, FIRST, inner, 0)

    @pl.when(below | (r < NG - 1))
    def _():
        pl.semaphore_wait(above_sem, NG - 1 - r + jnp.where(below, 1, 0))

    lax.fori_loop(0, NH, step_rows, 0)

    def step_last(h, carry):
        wait_bytes(zr.at[h, 1:], rz.at[h])
        up = jnp.where(above, zx[h, 0], 0.0)
        down = jnp.zeros((QT, DH), F32)
        for i in range(NG):
            up = up + jnp.where((r > i) & up_open[i], zr[h, i], 0.0)
            down = down + jnp.where((r < i) & down_open[i], zr[h, i], 0.0)
        for i in range(NX):
            p3[h, i, 0] = up
            up = p1[h, i, 0] + jnp.where(has_start[i], 0.0, up)
            back = NX - 1 - i
            p3[h, back, 1] = down
            down = p1[h, back, 1] + jnp.where(has_start[back], 0.0, down)

        @pl.when(above)
        def _():
            zx[h, 0] = down + zx[h, 1]
            zx[h, 1] = down
            for i in range(2):
                under_copy(h, i).start()

        for d in FAR_FIRST:
            part = below & (lax.rem(x + d, NX) >= NX - 2)

            @pl.when(~part)
            def _():
                last_copy(h, d).start()

            @pl.when(part)
            def _():
                last_part(h, d).start()

        st[h, 0, mine, :] = p3[h, x, 0]

        @pl.when(~begins)
        def _():
            st[h, 1, mine, :] = p3[h, x, 1]

        return carry

    lax.fori_loop(0, NH, step_last, 0)
    lax.fori_loop(FIRST, NH, inner, 0)

    wait_bytes(p1.at[:, 1:], s1)
    wait_bytes(zr.at[:, 1:], sz)

    @pl.when(below)
    def _():
        wait_bytes(zx, sx)

    def finish(h, carry):
        @pl.when(begins)
        def _():
            wait_bytes(p3.at[h, 1:, 0], r3.at[h])
            wait_bytes(st.at[h, 1], rw.at[h])

        @pl.when(~begins)
        def _():
            wait_bytes(p3.at[h, 1:], r3.at[h])

        columns = pl.ds(pl.multiple_of(h * DH, DH), DH)
        kv_in = [st[h, 0]]
        for c in range(NB - 1):
            kv_in.append(kvs[h, c] + jnp.where(chunk_start[c], 0.0, kv_in[-1]))
        qg_in = [st[h, 1]]
        for c in range(NB - 1, 0, -1):
            qg_in.insert(0, qgs[h, c] + jnp.where(chunk_start[c], 0.0, qg_in[0]))
        for c in range(NB):
            rows = pl.ds(TB * c, TB)
            kv_parts = split(kv_in[c])
            qg_parts = split(qg_in[c])
            kv_wide, kv_tall = (jnp.concatenate(kv_parts, axis=i) for i in (1, 0))
            qg_wide, qg_tall = (jnp.concatenate(qg_parts, axis=i) for i in (1, 0))
            twice = lambda a: jnp.concatenate([a[h, rows, :]] * 2, axis=1)
            head = head_b[rows, :]
            tail = tail_b[rows, :]
            o_att[rows, columns] = (pa[h, rows, :] + head * dot_nn(twice(q), kv_tall)).astype(BF16)
            o_gq[rows, columns] = (pb[h, rows, :] + head * dot_nt(twice(g), kv_wide)).astype(BF16)
            o_gk[rows, columns] = (pc[h, rows, :] + tail * dot_nt(twice(v), qg_wide)).astype(BF16)
            o_gv[rows, columns] = (pd[h, rows, :] + tail * dot_nn(twice(k), qg_tall)).astype(BF16)
        return carry

    lax.fori_loop(0, NH, finish, 0)

    @pl.when(~below)
    def _():
        wait_bytes(p3.at[:, 1:], s3)

    @pl.when(begins)
    def _():
        wait_bytes(p3.at[:, 2:], s3)
        wait_bytes(p3.at[:, 0, 0], s3_part)

    @pl.when(below & ~begins)
    def _():
        wait_bytes(p3.at[:, 0], s3)
        wait_bytes(p3.at[:, 2:, 0], s3_part)

    @pl.when(above)
    def _():
        wait_bytes(zx, sw)


def store_kernel(*refs):
    ins, outs, sem = refs[:4], refs[4:8], refs[8]
    copies = [pltpu.make_async_copy(a, b, sem.at[i]) for i, (a, b) in enumerate(zip(ins, outs))]
    for copy in copies:
        copy.start()
    for copy in copies:
        copy.wait()


def per_device(query_rows, key_rows, value_rows, grad_out, doc_lengths):
    whole = pl.BlockSpec(memory_space=pltpu.HBM)
    in_vmem = pl.BlockSpec(memory_space=pltpu.VMEM)
    wide = (T, NH * DH)
    heads = (NH, T, DH)
    dma = pltpu.SemaphoreType.DMA
    results = pl.pallas_call(
        fused_kernel,
        name="attend",
        out_shape=[pltpu.VMEM(wide, BF16)] * 4,
        in_specs=[whole] * 5,
        out_specs=[in_vmem] * 4,
        scratch_shapes=[pltpu.VMEM((NH, 4, T, DH), BF16), pltpu.VMEM(heads, BF16)]
        + [pltpu.VMEM(heads, F32)] * 4
        + [
            pltpu.VMEM((NH, NB, DH, DH), F32),
            pltpu.VMEM((NH, NB, DH, DH), F32),
            pltpu.VMEM((NH, 2, DH, DH), F32),
            pltpu.VMEM((NH, NX, 2, QT, DH), F32),
            pltpu.VMEM((NH, 3, QT, DH), F32),
            pltpu.VMEM((NH, NG, QT, DH), F32),
            pltpu.VMEM((NH, 2, QT, DH), F32),
            pltpu.VMEM((NH, NX, 2, QT, DH), F32),
            pltpu.VMEM((NH, 2, DH, DH), F32),
            pltpu.VMEM((T, DH), F32),
            pltpu.VMEM((T, DH), F32),
            pltpu.VMEM((T, DH), F32),
            pltpu.VMEM((T, DH), BF16),
            pltpu.VMEM((T, DH), jnp.int32),
            pltpu.SMEM((DOCS,), jnp.int32),
            dma,
            pltpu.SemaphoreType.REGULAR,
            dma((NH,)),
            dma,
            dma((NH,)),
            dma,
            dma((NH,)),
            dma,
            dma((NH,)),
            dma,
            dma((NH,)),
            dma,
            dma,
            dma((NH,)),
        ],
        compiler_params=pltpu.CompilerParams(
            collective_id=0, has_side_effects=True, vmem_limit_bytes=40 << 20
        ),
    )(*(
        pltpu.with_memory_space_constraint(a, pltpu.HBM)
        for a in (doc_lengths, query_rows, key_rows, value_rows, grad_out)
    ))
    return tuple(
        pl.pallas_call(
            store_kernel,
            name="store",
            out_shape=[jax.ShapeDtypeStruct(wide, BF16)] * 4,
            in_specs=[in_vmem] * 4,
            out_specs=[whole] * 4,
            scratch_shapes=[dma((4,))],
            compiler_params=pltpu.CompilerParams(vmem_limit_bytes=8 << 20),
        )(*results)
    )


def solution(mesh):
    placed = (P("seq", "head"), P("seq", "head"), P("seq", "head"), P("seq", "head"), P())
    return jax.shard_map(
        per_device,
        mesh=mesh,
        in_specs=placed,
        out_specs=(P("seq", "head"), P("seq", "head"), P("seq", "head"), P("seq", "head")),
        check_vma=False,
    )
```

```python
import functools

import jax
import jax.numpy as jnp
from jax import lax
from jax.experimental import pallas as pl
from jax.experimental.pallas import tpu as pltpu
from jax.sharding import PartitionSpec as P

MESH = pl.DeviceIdType.MESH
DH = 128
T = 768
NH = 4
DOCS = 16
NX = 4
QT = DH // NX
TB = 256
NB = T // TB
FIRST = 3
FAR_FIRST = (2, 1, 3)
LAST_ROW = 3
NG = 4
F32 = jnp.float32
BF16 = jnp.bfloat16


def dot_nn(a, b):
    return lax.dot_general(a, b, (((1,), (0,)), ((), ())), preferred_element_type=F32)


def dot_nt(a, b):
    return lax.dot_general(a, b, (((1,), (1,)), ((), ())), preferred_element_type=F32)


def dot_tn(a, b):
    return lax.dot_general(a, b, (((0,), (0,)), ((), ())), preferred_element_type=F32)


def split(a):
    high = a.astype(BF16)
    return high, (a - high.astype(F32)).astype(BF16)


def fused_kernel(
    len_hbm, q_hbm, k_hbm, v_hbm, g_hbm, o_att, o_gq, o_gk, o_gv,
    ins, pa, pb, pc, pd, kvs, qgs, loc, p1, zs, zr, zx, p3, st,
    rs_b, head_b, tail_b, tail_low, first_b,
    len_ref, len_sem, above_sem, in_sem, s1, r1, sz, rz, sx, rx, sw, rw, s3, s3_part, r3,
):
    q, k, v, g = (ins.at[:, i] for i in range(4))
    seq = lax.axis_index("seq")
    z = seq // NX
    x = seq % NX
    offset = seq * T
    base = (z // NG) * NG
    r = z - base
    below = z == NG - 1
    above = z == NG
    begins = below & (x >= NX - 2)

    def peer_x(d):
        return {"seq": z * NX + lax.rem(x + d, NX)}

    def peer_row(d):
        return lax.rem(r + d, NG)

    def peer_z(d):
        return {"seq": (base + peer_row(d)) * NX + x}

    def wait_bytes(ref, sem):
        pltpu.make_async_copy(ref, ref, sem).wait()

    lengths = pltpu.make_async_copy(len_hbm, len_ref, len_sem)
    lengths.start()

    barrier = pltpu.get_barrier_semaphore()
    for d in range(1, NX):
        pl.semaphore_signal(barrier, inc=1, device_id=peer_x(d), device_id_type=MESH)
    for d in range(1, NG):
        @pl.when(peer_row(d) > r)
        def _():
            pl.semaphore_signal(barrier, inc=1, device_id=peer_z(d), device_id_type=MESH)

    @pl.when(below)
    def _():
        up = {"seq": NG * NX + x}
        pl.semaphore_signal(barrier, inc=1, device_id=up, device_id_type=MESH)

    @pl.when(begins)
    def _():
        for d in range(1, NX):
            beside = {"seq": NG * NX + lax.rem(x + d, NX)}
            pl.semaphore_signal(barrier, inc=1, device_id=beside, device_id_type=MESH)

    def fetches(h):
        columns = pl.ds(pl.multiple_of(h * DH, DH), DH)
        return [
            pltpu.make_async_copy(src.at[:, columns], ins.at[h, i], in_sem.at[h])
            for i, src in enumerate((q_hbm, k_hbm, v_hbm, g_hbm))
        ]

    for h in range(NH):
        for copy in fetches(h):
            copy.start()

    lengths.wait()
    starts = [jnp.int32(0)]
    for j in range(DOCS - 1):
        starts.append(starts[-1] + len_ref[j])

    def last_start_before(limit):
        found = jnp.int32(0)
        for j in range(1, DOCS):
            found = jnp.where(starts[j] < limit, starts[j], found)
        return found

    row = z * (NX * T)
    has_start = [
        last_start_before(row + (i + 1) * T) >= row + i * T for i in range(NX)
    ]
    before_row = last_start_before(row)
    up_open = [before_row < (base + i + 1) * NX * T for i in range(NG)]
    down_open = [last_start_before((base + i) * NX * T) < row + NX * T for i in range(NG)]

    def first_of(place):
        first = jnp.full(place.shape, -offset, jnp.int32)
        for j in range(1, DOCS):
            local = starts[j] - offset
            first = jnp.where(place >= local, local, first)
        return first, lax.rsqrt((place - first + 1).astype(F32) * DH)

    chunk_start = []
    for c in range(NB):
        from_here = last_start_before(offset + TB * (c + 1)) - offset
        chunk_start.append(from_here >= TB * c)
        for top in range(TB * c, TB * (c + 1), DH):
            rows = pl.ds(top, DH)
            place = lax.broadcasted_iota(jnp.int32, (DH, DH), 0) + top
            first, scale = first_of(place)
            first_b[rows, :] = first
            rs_b[rows, :] = scale
            head_b[rows, :] = jnp.where(first < TB * c, scale, 0.0)
            tails = jnp.where(place >= from_here, 1.0, 0.0)
            tail_b[rows, :] = tails
            tail_low[rows, :] = tails.astype(BF16)

    from_below = jnp.where(above, jnp.where(x >= NX - 2, 2, 3), r)
    pl.semaphore_wait(barrier, NX - 1 + from_below)
    for d in range(1, NG):
        @pl.when(peer_row(d) < r)
        def _():
            pl.semaphore_signal(above_sem, inc=1, device_id=peer_z(d), device_id_type=MESH)

    @pl.when(above)
    def _():
        down = {"seq": (NG - 1) * NX + x}
        pl.semaphore_signal(above_sem, inc=1, device_id=down, device_id_type=MESH)

    def first_copy(h, d):
        target = lax.rem(x + d, NX)
        return pltpu.make_async_remote_copy(
            loc.at[h, :, pl.ds(pl.multiple_of(target * QT, QT), QT), :],
            p1.at[h, x],
            s1,
            r1.at[h],
            device_id=peer_x(d),
            device_id_type=MESH,
        )

    def row_copy(h, d):
        return pltpu.make_async_remote_copy(
            zs.at[h, jnp.where(peer_row(d) > r, 1, 0)],
            zr.at[h, r],
            sz,
            rz.at[h],
            device_id=peer_z(d),
            device_id_type=MESH,
        )

    def over_copy(h):
        return pltpu.make_async_remote_copy(
            zs.at[h, 1:3],
            zx.at[h],
            sx,
            rx.at[h],
            device_id={"seq": NG * NX + x},
            device_id_type=MESH,
        )

    def under_copy(h, i):
        return pltpu.make_async_remote_copy(
            zx.at[h, i],
            st.at[h, 1, mine, :],
            sw,
            rw.at[h],
            device_id={"seq": (NG - 1) * NX + NX - 2 + i},
            device_id_type=MESH,
        )

    def last_copy(h, d):
        return pltpu.make_async_remote_copy(
            p3.at[h, lax.rem(x + d, NX)],
            st.at[h, :, mine, :],
            s3,
            r3.at[h],
            device_id=peer_x(d),
            device_id_type=MESH,
        )

    def last_part(h, d):
        return pltpu.make_async_remote_copy(
            p3.at[h, lax.rem(x + d, NX), 0],
            st.at[h, 0, mine, :],
            s3_part,
            r3.at[h],
            device_id=peer_x(d),
            device_id_type=MESH,
        )

    mine = pl.ds(pl.multiple_of(x * QT, QT), QT)

    def states(h, carry):
        wait_bytes(ins.at[h], in_sem.at[h])
        for c in range(NB):
            rows = pl.ds(TB * c, TB)
            kvs[h, c] = dot_tn(k[h, rows, :], v[h, rows, :] * tail_low[rows, :])
            gf = g[h, rows, :].astype(F32)
            high_part, low_part = split(head_b[rows, :] * gf)
            both = dot_tn(q[h, rows, :], jnp.concatenate([high_part, low_part], axis=1))
            qgs[h, c] = both[:, :DH] + both[:, DH:]
        up = kvs[h, 0]
        down = qgs[h, NB - 1]
        for c in range(1, NB):
            up = kvs[h, c] + jnp.where(chunk_start[c], 0.0, up)
            back = NB - 1 - c
            down = qgs[h, back] + jnp.where(chunk_start[back], 0.0, down)
        loc[h, 0] = up
        loc[h, 1] = down
        for d in FAR_FIRST:
            first_copy(h, d).start()
        p1[h, x] = loc[h, :, mine, :]
        return carry

    lax.fori_loop(0, NH, states, 0)

    def inside(h):
        for c in range(NB):
            rows = pl.ds(TB * c, TB)
            qc, kc, vc, gc = (a[h, rows, :] for a in (q, k, v, g))
            over = lambda a: jnp.concatenate([a] * (TB // DH), axis=1)
            high = lax.broadcasted_iota(jnp.int32, (TB, TB), 0)
            wide = lax.broadcasted_iota(jnp.int32, (TB, TB), 1)
            seen = (wide + TB * c >= over(first_b[rows, :])) & (wide <= high)
            rs = rs_b[rows, :]
            scores = jnp.where(seen, dot_nt(qc, kc), 0.0).astype(BF16)
            grads = jnp.where(seen, dot_nt(gc, vc) * over(rs), 0.0).astype(BF16)
            pa[h, rows, :] = rs * dot_nn(scores, vc)
            pb[h, rows, :] = dot_nn(grads, kc)
            low = (rs * gc.astype(F32)).astype(BF16)
            pd[h, rows, :] = dot_tn(scores, low)
            pc[h, rows, :] = dot_tn(grads, qc)

    def step_rows(h, carry):
        wait_bytes(p1.at[h, 1:], r1.at[h])
        up = p1[h, 0, 0]
        down = p1[h, NX - 1, 1]
        for i in range(1, NX):
            up = p1[h, i, 0] + jnp.where(has_start[i], 0.0, up)
            back = NX - 1 - i
            down = p1[h, back, 1] + jnp.where(has_start[back], 0.0, down)
        zs[h, 0] = down
        zs[h, 1] = up
        zs[h, 2] = p1[h, NX - 1, 1]

        @pl.when(below)
        def _():
            over_copy(h).start()

        @pl.when(above)
        def _():
            wait_bytes(zx.at[h], rx.at[h])
            zs[h, 1] = zs[h, 1] + zx[h, 0]

        for d in range(1, NG):
            row_copy(h, d).start()
        return carry

    def inner(h, carry):
        inside(h)
        return carry

    lax.fori_loop(0, FIRST, inner, 0)

    @pl.when(below | (r < NG - 1))
    def _():
        pl.semaphore_wait(above_sem, NG - 1 - r + jnp.where(below, 1, 0))

    lax.fori_loop(0, NH, step_rows, 0)

    def step_last(h, carry):
        wait_bytes(zr.at[h, 1:], rz.at[h])
        up = jnp.where(above, zx[h, 0], 0.0)
        down = jnp.zeros((QT, DH), F32)
        for i in range(NG):
            up = up + jnp.where((r > i) & up_open[i], zr[h, i], 0.0)
            down = down + jnp.where((r < i) & down_open[i], zr[h, i], 0.0)
        for i in range(NX):
            p3[h, i, 0] = up
            up = p1[h, i, 0] + jnp.where(has_start[i], 0.0, up)
            back = NX - 1 - i
            p3[h, back, 1] = down
            down = p1[h, back, 1] + jnp.where(has_start[back], 0.0, down)

        @pl.when(above)
        def _():
            zx[h, 0] = down + zx[h, 1]
            zx[h, 1] = down
            for i in range(2):
                under_copy(h, i).start()

        for d in FAR_FIRST:
            part = below & (lax.rem(x + d, NX) >= NX - 2)

            @pl.when(~part)
            def _():
                last_copy(h, d).start()

            @pl.when(part)
            def _():
                last_part(h, d).start()

        st[h, 0, mine, :] = p3[h, x, 0]

        @pl.when(~begins)
        def _():
            st[h, 1, mine, :] = p3[h, x, 1]

        return carry

    lax.fori_loop(0, NH, step_last, 0)
    lax.fori_loop(FIRST, NH, inner, 0)

    wait_bytes(p1.at[:, 1:], s1)
    wait_bytes(zr.at[:, 1:], sz)

    @pl.when(below)
    def _():
        wait_bytes(zx, sx)

    def finish(h, carry):
        @pl.when(begins)
        def _():
            wait_bytes(p3.at[h, 1:, 0], r3.at[h])
            wait_bytes(st.at[h, 1], rw.at[h])

        @pl.when(~begins)
        def _():
            wait_bytes(p3.at[h, 1:], r3.at[h])

        columns = pl.ds(pl.multiple_of(h * DH, DH), DH)
        kv_in = [st[h, 0]]
        for c in range(NB - 1):
            kv_in.append(kvs[h, c] + jnp.where(chunk_start[c], 0.0, kv_in[-1]))
        qg_in = [st[h, 1]]
        for c in range(NB - 1, 0, -1):
            qg_in.insert(0, qgs[h, c] + jnp.where(chunk_start[c], 0.0, qg_in[0]))
        for c in range(NB):
            rows = pl.ds(TB * c, TB)
            kv_parts = split(kv_in[c])
            qg_parts = split(qg_in[c])
            kv_wide, kv_tall = (jnp.concatenate(kv_parts, axis=i) for i in (1, 0))
            qg_wide, qg_tall = (jnp.concatenate(qg_parts, axis=i) for i in (1, 0))
            twice = lambda a: jnp.concatenate([a[h, rows, :]] * 2, axis=1)
            head = head_b[rows, :]
            tail = tail_b[rows, :]
            o_att[rows, columns] = (pa[h, rows, :] + head * dot_nn(twice(q), kv_tall)).astype(BF16)
            o_gq[rows, columns] = (pb[h, rows, :] + head * dot_nt(twice(g), kv_wide)).astype(BF16)
            o_gk[rows, columns] = (pc[h, rows, :] + tail * dot_nt(twice(v), qg_wide)).astype(BF16)
            o_gv[rows, columns] = (pd[h, rows, :] + tail * dot_nn(twice(k), qg_tall)).astype(BF16)
        return carry

    lax.fori_loop(0, NH, finish, 0)

    @pl.when(~below)
    def _():
        wait_bytes(p3.at[:, 1:], s3)

    @pl.when(begins)
    def _():
        wait_bytes(p3.at[:, 2:], s3)
        wait_bytes(p3.at[:, 0, 0], s3_part)

    @pl.when(below & ~begins)
    def _():
        wait_bytes(p3.at[:, 0], s3)
        wait_bytes(p3.at[:, 2:, 0], s3_part)

    @pl.when(above)
    def _():
        wait_bytes(zx, sw)


def store_kernel(*refs):
    ins, outs, sem = refs[:4], refs[4:8], refs[8]
    copies = [pltpu.make_async_copy(a, b, sem.at[i]) for i, (a, b) in enumerate(zip(ins, outs))]
    for copy in copies:
        copy.start()
    for copy in copies:
        copy.wait()


def per_device(query_rows, key_rows, value_rows, grad_out, doc_lengths):
    whole = pl.BlockSpec(memory_space=pltpu.HBM)
    in_vmem = pl.BlockSpec(memory_space=pltpu.VMEM)
    wide = (T, NH * DH)
    heads = (NH, T, DH)
    dma = pltpu.SemaphoreType.DMA
    results = pl.pallas_call(
        fused_kernel,
        name="attend",
        out_shape=[pltpu.VMEM(wide, BF16)] * 4,
        in_specs=[whole] * 5,
        out_specs=[in_vmem] * 4,
        scratch_shapes=[pltpu.VMEM((NH, 4, T, DH), BF16)]
        + [pltpu.VMEM(heads, F32)] * 4
        + [
            pltpu.VMEM((NH, NB, DH, DH), F32),
            pltpu.VMEM((NH, NB, DH, DH), F32),
            pltpu.VMEM((NH, 2, DH, DH), F32),
            pltpu.VMEM((NH, NX, 2, QT, DH), F32),
            pltpu.VMEM((NH, 3, QT, DH), F32),
            pltpu.VMEM((NH, NG, QT, DH), F32),
            pltpu.VMEM((NH, 2, QT, DH), F32),
            pltpu.VMEM((NH, NX, 2, QT, DH), F32),
            pltpu.VMEM((NH, 2, DH, DH), F32),
            pltpu.VMEM((T, DH), F32),
            pltpu.VMEM((T, DH), F32),
            pltpu.VMEM((T, DH), F32),
            pltpu.VMEM((T, DH), BF16),
            pltpu.VMEM((T, DH), jnp.int32),
            pltpu.SMEM((DOCS,), jnp.int32),
            dma,
            pltpu.SemaphoreType.REGULAR,
            dma((NH,)),
            dma,
            dma((NH,)),
            dma,
            dma((NH,)),
            dma,
            dma((NH,)),
            dma,
            dma((NH,)),
            dma,
            dma,
            dma((NH,)),
        ],
        compiler_params=pltpu.CompilerParams(
            collective_id=0, has_side_effects=True, vmem_limit_bytes=40 << 20
        ),
    )(*(
        pltpu.with_memory_space_constraint(a, pltpu.HBM)
        for a in (doc_lengths, query_rows, key_rows, value_rows, grad_out)
    ))
    return tuple(
        pl.pallas_call(
            store_kernel,
            name="store",
            out_shape=[jax.ShapeDtypeStruct(wide, BF16)] * 4,
            in_specs=[in_vmem] * 4,
            out_specs=[whole] * 4,
            scratch_shapes=[dma((4,))],
            compiler_params=pltpu.CompilerParams(vmem_limit_bytes=8 << 20),
        )(*results)
    )


def solution(mesh):
    placed = (P("seq", "head"), P("seq", "head"), P("seq", "head"), P("seq", "head"), P())
    return jax.shard_map(
        per_device,
        mesh=mesh,
        in_specs=placed,
        out_specs=(P("seq", "head"), P("seq", "head"), P("seq", "head"), P("seq", "head")),
        check_vma=False,
    )
```
